256 devices in a mesh: section: 64 (over x, z, core), head: 4 (over y).
Axes of the slice: x: 4, y: 4, z: 8, core: 2. Of those that a mesh axis runs over, the one named last changes fastest.
Arguments:
- state: bfloat16 [64, 256, 3072], P('section', None, 'head'), may hold values from -6 to 6
- modulation: float32 [64, 3, 3072], P('section'), may hold values from -3 to 3
- w_qkv: bfloat16 [64, 3072, 3, 1536], P('section', None, None, 'head'), may hold values from -0.109375 to 0.109375
- w_out: bfloat16 [64, 1536, 3072], P('section', 'head'), may hold values from -0.15625 to 0.15625
- stale_kv: bfloat16 [64, 2, 1152, 1536], P('section', None, None, 'head'), may hold values from -4 to 4
- patch_order: int32 [4], replicated, may hold values from 0 to 3, each once
- text_count: int32 [1], replicated, may hold values from 32 to 128
Outputs:
- state_out: bfloat16 [64, 256, 3072], P('section', None, 'head')
- fresh_kv: bfloat16 [64, 2, 2, 256, 1536], P('section', None, None, None, 'head')
The draws below stay inside these ranges and needn't reach their ends.
Inputs may be any that keep to these rules, and one draw needn't show every extreme that they name: `patch_order`: each patch once.
All inputs are finite; a program needn't handle non-finite values.
Results may differ from the reference program's by a relative error of at most 0.01.
Values may be sent and summed in bfloat16 or wider, within the bound.
A program may use at most 128 MiB of HBM per device.

```python
import jax
import jax.numpy as jnp
from jax import lax

D = 3072
HEADS = 12
HEAD_DIM = 128
PATCH = 256
PATCHES = 4
TEXT = 128
TICKS = 2
LAYERS = 64
KEYS = 1152
INNER = 1536
N_HEAD = 4


def level_of(own_key, extent, shards, least, top_value):
    def one(position, parts):
        heights = jax.random.uniform(jax.random.fold_in(jax.random.fold_in(own_key, 6), position), (parts,), jnp.float32, least / len(shards), top_value / len(shards))
        return jnp.repeat(jnp.exp(heights), extent[position] // parts).reshape((-1,) + (1,) * (len(extent) - position - 1))

    loudness = one(*shards[0])
    for cut in shards[1:]:
        loudness = loudness * one(*cut)
    return loudness


def gaussian(own_key, extent, scale, most, shards=(), kind=jnp.bfloat16):
    entries = scale * jax.random.normal(own_key, extent, jnp.float32)
    if shards:
        entries = entries * level_of(own_key, extent, shards, -0.22, 0.18)
    return jnp.clip(entries, -most, most).astype(kind)


def setup_inputs(seed: int = 0) -> dict:
    splits = jax.random.split(jax.random.key(seed), 8)
    return {
        "state": gaussian(splits[0], (LAYERS, PATCH, D), 1.0, 6.0, ((0, 64), (2, 4))),
        "modulation": gaussian(splits[1], (LAYERS, 3, D), 0.5, 3.0, ((0, 64),), jnp.float32),
        "w_qkv": gaussian(splits[2], (LAYERS, D, 3, INNER), D ** -0.5, 0.109375, ((0, 64), (3, 4))),
        "w_out": gaussian(splits[3], (LAYERS, INNER, D), INNER ** -0.5, 0.15625, ((0, 64), (1, 4))),
        "stale_kv": gaussian(splits[4], (LAYERS, 2, KEYS, INNER), 1.0, 4.0, ((0, 64), (3, 4))),
        "patch_order": jax.random.permutation(splits[5], PATCHES).astype(jnp.int32),
        "text_count": jax.random.randint(splits[6], (1,), TEXT // 4, TEXT + 1).astype(jnp.int32),
    }


epsilon = 1e-06

def modulate(states, shift_row, scale_row):
    widened = states.astype(jnp.float32)
    centre = lax.optimization_barrier(jnp.mean(widened, axis=-1, keepdims=True))
    spread = lax.optimization_barrier(jnp.mean((widened - centre) ** 2, axis=-1, keepdims=True))
    normed = (widened - centre) * lax.rsqrt(spread + epsilon) * (1.0 + scale_row) + shift_row
    return normed.astype(jnp.bfloat16)

def head_norm(columns, head_count):
    shaped = columns.reshape(columns.shape[0], head_count, HEAD_DIM)
    squares = lax.optimization_barrier(jnp.mean(shaped * shaped, axis=-1, keepdims=True))
    return (shaped * lax.rsqrt(squares + epsilon)).astype(jnp.bfloat16)

def apply_layer(layer_index, moment, states, factors, qkv_weight, out_weight, caches, patch_order, text_count):
    slot_index = jnp.mod(moment - layer_index, PATCHES)
    first_row = (TEXT + patch_order[slot_index] * PATCH).astype(jnp.int32)
    zero_col = jnp.zeros((), jnp.int32)
    normed = modulate(states, factors[0], factors[1])
    projected = jnp.dot(normed, qkv_weight.reshape(D, 3 * INNER), preferred_element_type=jnp.float32)
    queries = head_norm(projected[:, :INNER], HEADS)
    new_keys = head_norm(projected[:, INNER:2 * INNER], HEADS).reshape(PATCH, INNER)
    new_values = projected[:, 2 * INNER:].astype(jnp.bfloat16)
    all_keys = lax.dynamic_update_slice(caches[0], new_keys, (first_row, zero_col))
    all_values = lax.dynamic_update_slice(caches[1], new_values, (first_row, zero_col))
    scores = jnp.einsum('phd,khd->hpk', queries.astype(jnp.float32), all_keys.reshape(KEYS, HEADS, HEAD_DIM).astype(jnp.float32)) * HEAD_DIM ** (-0.5)
    positions = jnp.arange(KEYS)
    visible = (positions < text_count[0]) | (positions >= TEXT)
    exponent = jnp.where(visible[None, None, :], jnp.exp(scores), 0.0)
    totals = lax.optimization_barrier(jnp.sum(exponent, axis=-1))
    rounded = exponent.astype(jnp.bfloat16)
    mixed = jnp.einsum('hpk,khd->phd', rounded.astype(jnp.float32), all_values.reshape(KEYS, HEADS, HEAD_DIM).astype(jnp.float32))
    attended = (mixed / jnp.transpose(totals)[:, :, None]).astype(jnp.bfloat16)
    grouped = attended.reshape(PATCH, N_HEAD, INNER // N_HEAD).astype(jnp.float32)
    group_weight = out_weight.reshape(N_HEAD, INNER // N_HEAD, D).astype(jnp.float32)
    terms = jnp.einsum('pgc,gcd->gpd', grouped, group_weight).astype(jnp.bfloat16)
    terms = lax.optimization_barrier(terms)
    summed = lax.optimization_barrier(jnp.sum(terms.astype(jnp.float32), axis=0))
    updated = (states.astype(jnp.float32) + factors[2] * summed).astype(jnp.bfloat16)
    fresh_pair = jnp.stack([new_keys, new_values])
    new_cache = jnp.stack([all_keys, all_values])
    return (updated, fresh_pair, new_cache)

def reference(state, modulation, w_qkv, w_out, stale_kv, patch_order, text_count):
    states = state
    caches = stale_kv
    fresh_list = []
    for moment in range(TICKS):

        def run_layer(packed):
            layer_index, layer_state, factors, qkv_weight, out_weight, layer_cache = packed
            return apply_layer(layer_index, moment, layer_state, factors, qkv_weight, out_weight, layer_cache, patch_order, text_count)
        updated, fresh_pair, caches = lax.map(run_layer, (jnp.arange(LAYERS, dtype=jnp.int32), states, modulation, w_qkv, w_out, caches))
        fresh_list.append(fresh_pair)
        states = jnp.roll(updated, 1, axis=0)
    return (states, jnp.stack(fresh_list, axis=1))
```

```python
import functools

import jax
import jax.numpy as jnp
from jax import lax
from jax.experimental import pallas as pl
from jax.experimental.pallas import tpu as pltpu
from jax.sharding import PartitionSpec as P

MESH = pl.DeviceIdType.MESH
HEAD_DIM = 128
TICKS = 2
EPSILON = 1e-06
CHUNKS = 4

(
    OWN_RIGHT,
    OWN_LEFT,
    PASS_RIGHT,
    PASS_LEFT,
    FAR_RIGHT,
    FAR_LEFT,
    PLAIN_RIGHT,
    PLAIN_LEFT,
    SUM_RIGHT,
    SUM_LEFT,
    SHIFT,
    KINDS,
) = range(12)


def kernel(
    sections,
    order_ref,
    count_ref,
    state_ref,
    mod_ref,
    wqkv_ref,
    wout_ref,
    stale_ref,
    out_ref,
    fresh_ref,
    rows_buf,
    terms,
    far_buf,
    near_buf,
    y_buf,
    mod,
    wqkv,
    wout,
    stale,
    q_buf,
    k_buf,
    v_buf,
    local_sem,
    send_sem,
    recv_sem,
):
    section = lax.axis_index("section")
    y = lax.axis_index("head")
    ny = 4
    right, left, across = lax.rem(y + 1, ny), lax.rem(y + 3, ny), lax.rem(y + 2, ny)
    behind = lax.rem(section + sections - 1, sections)
    ahead = lax.rem(section + 1, sections)
    to_right, to_left, to_ahead = (section, right), (section, left), (ahead, y)

    patch, share = state_ref.shape
    inner = wout_ref.shape[0]
    heads = inner // HEAD_DIM
    keys = stale_ref.shape[1]
    text = keys - 4 * patch
    width = ny * share
    size = patch // CHUNKS
    half = size // 2

    state_in = pltpu.make_async_copy(state_ref, rows_buf.at[0, y], local_sem.at[0])
    mod_in = pltpu.make_async_copy(mod_ref, mod, local_sem.at[1])
    stale_in = pltpu.make_async_copy(stale_ref, stale, local_sem.at[2])
    wqkv_in = pltpu.make_async_copy(wqkv_ref, wqkv, local_sem.at[3])
    wout_in = pltpu.make_async_copy(wout_ref, wout, local_sem.at[4])
    for copy in (state_in, mod_in, stale_in, wqkv_in, wout_in):
        copy.start()

    barrier = pltpu.get_barrier_semaphore()
    for target in (to_right, to_left, (behind, y)):
        pl.semaphore_signal(barrier, inc=1, device_id=target, device_id_type=MESH)
    pl.semaphore_wait(barrier, 3)

    def rows_of(c, start=0, count=size):
        return pl.ds(pl.multiple_of(c * size + start, 16), count)

    def remote(t, c, kind, source, target, device):
        return pltpu.make_async_remote_copy(
            src_ref=source,
            dst_ref=target,
            send_sem=send_sem.at[t, c, kind],
            recv_sem=recv_sem.at[t, c, kind],
            device_id=device,
            device_id_type=MESH,
        )

    def own_copy(t, c, kind, who, device):
        ref = rows_buf.at[t, who, rows_of(c)]
        return remote(t, c, kind, ref, ref, device)

    def pass_copy(t, c, kind, who, device):
        start = 0 if kind == PASS_RIGHT else half
        ref = rows_buf.at[t, who, rows_of(c, start, half)]
        return remote(t, c, kind, ref, ref, device)

    def far_copy(t, c, kind, who, device):
        side = 0 if kind == FAR_RIGHT else 1
        start = 0 if kind == FAR_RIGHT else half
        return remote(
            t,
            c,
            kind,
            terms.at[t, who, rows_of(c, start, half)],
            far_buf.at[t, side, pl.ds(pl.multiple_of(c * half, 16), half)],
            device,
        )

    def near_copy(t, c, kind, who, device):
        side = 0 if kind in (PLAIN_RIGHT, SUM_RIGHT) else 1
        start = 0 if kind in (SUM_RIGHT, PLAIN_LEFT) else half
        return remote(
            t,
            c,
            kind,
            terms.at[t, who, rows_of(c, start, half)],
            near_buf.at[t, side, rows_of(c, start, half)],
            device,
        )

    def shift_copy(t, c):
        if t + 1 < TICKS:
            target = rows_buf.at[t + 1, y, rows_of(c)]
        else:
            target = out_ref.at[rows_of(c)]
        return remote(t, c, SHIFT, y_buf.at[t, rows_of(c)], target, to_ahead)

    def gather_send(t, c):
        own_copy(t, c, OWN_RIGHT, y, to_right).start()
        own_copy(t, c, OWN_LEFT, y, to_left).start()

    def gather_pass(t, c):
        own_copy(t, c, OWN_RIGHT, left, to_right).wait_recv()
        pass_copy(t, c, PASS_RIGHT, left, to_right).start()
        own_copy(t, c, OWN_LEFT, right, to_left).wait_recv()
        pass_copy(t, c, PASS_LEFT, right, to_left).start()

    def project(t, c):
        pass_copy(t, c, PASS_RIGHT, across, to_right).wait_recv()
        pass_copy(t, c, PASS_LEFT, across, to_left).wait_recv()
        total = jnp.zeros((size, 1), jnp.float32)
        parts = []
        for j in range(ny):
            part = rows_buf[t, j, rows_of(c)].astype(jnp.float32)
            total += jnp.sum(part, axis=-1, keepdims=True)
            parts.append(part)
        centre = total * (1.0 / width)
        spread = jnp.zeros((size, 1), jnp.float32)
        for j in range(ny):
            gap = parts[j] - centre
            spread += jnp.sum(gap * gap, axis=-1, keepdims=True)
        factor = lax.rsqrt(spread * (1.0 / width) + EPSILON)
        sums = [jnp.zeros((size, inner), jnp.float32) for _ in range(3)]
        for j in range(ny):
            columns = slice(j * share, (j + 1) * share)
            part = rows_buf[t, j, rows_of(c)].astype(jnp.float32)
            normed = (part - centre) * factor * (1.0 + mod[1, :, columns]) + mod[0, :, columns]
            normed = normed.astype(jnp.bfloat16)
            for s in range(3):
                sums[s] += jnp.dot(
                    normed, wqkv[s, columns, :], preferred_element_type=jnp.float32
                )
        place = pl.ds(pl.multiple_of(fresh_row(t) + c * size, 16), size)
        for h in range(heads):
            columns = slice(h * HEAD_DIM, (h + 1) * HEAD_DIM)
            for s, target, where in ((0, q_buf, rows_of(c)), (1, k_buf, place)):
                value = sums[s][:, columns]
                square = jnp.mean(value * value, axis=-1, keepdims=True)
                target[where, columns] = (value * lax.rsqrt(square + EPSILON)).astype(jnp.bfloat16)
            v_buf[place, 2 * h * HEAD_DIM : (2 * h + 1) * HEAD_DIM] = sums[2][:, columns].astype(
                jnp.bfloat16
            )

    def fresh_row(t):
        return text + 3 * patch + t * patch

    def attend(t, c):
        window = slice(t * patch, t * patch + keys)
        text_at = patch if t == 0 else 0
        position = lax.broadcasted_iota(jnp.int32, (size, text), 1)
        alive = position < count_ref[0]
        mixed = []
        for h in range(heads):
            columns = slice(h * HEAD_DIM, (h + 1) * HEAD_DIM)
            scores = lax.dot_general(
                q_buf[rows_of(c), columns],
                k_buf[window, columns],
                (((1,), (1,)), ((), ())),
                preferred_element_type=jnp.float32,
            )
            weights = jnp.exp(scores * HEAD_DIM ** (-0.5))
            pieces = [jnp.where(alive, weights[:, text_at : text_at + text], 0.0)]
            if text_at:
                pieces.insert(0, weights[:, :text_at])
            pieces.append(weights[:, text_at + text :])
            weights = jnp.concatenate(pieces, axis=1).astype(jnp.bfloat16)
            both = jnp.dot(
                weights,
                v_buf[window, 2 * h * HEAD_DIM : 2 * (h + 1) * HEAD_DIM],
                preferred_element_type=jnp.float32,
            )
            mixed.append((both[:, :HEAD_DIM] / both[:, HEAD_DIM:]).astype(jnp.bfloat16))
        mixed = jnp.concatenate(mixed, axis=1)
        for j in range(ny):
            columns = slice(j * share, (j + 1) * share)
            terms[t, j, rows_of(c)] = jnp.dot(
                mixed, wout[:, columns], preferred_element_type=jnp.float32
            ).astype(jnp.bfloat16)
        far_copy(t, c, FAR_RIGHT, across, to_right).start()
        far_copy(t, c, FAR_LEFT, across, to_left).start()
        near_copy(t, c, PLAIN_RIGHT, right, to_right).start()
        near_copy(t, c, PLAIN_LEFT, left, to_left).start()

    def combine(t, c):
        for far, near, who, device, side, start in (
            (FAR_RIGHT, SUM_RIGHT, right, to_right, 0, 0),
            (FAR_LEFT, SUM_LEFT, left, to_left, 1, half),
        ):
            far_copy(t, c, far, who, device).wait_recv()
            rows = rows_of(c, start, half)
            arrived = far_buf[t, side, pl.ds(pl.multiple_of(c * half, 16), half)]
            terms[t, who, rows] = (
                terms[t, who, rows].astype(jnp.float32) + arrived.astype(jnp.float32)
            ).astype(jnp.bfloat16)
            near_copy(t, c, near, who, device).start()

    def finish(t, c):
        for kind in (PLAIN_RIGHT, PLAIN_LEFT, SUM_RIGHT, SUM_LEFT):
            device = to_right if kind in (PLAIN_RIGHT, SUM_RIGHT) else to_left
            near_copy(t, c, kind, y, device).wait_recv()
        rows = rows_of(c)
        total = terms[t, y, rows].astype(jnp.float32)
        total += near_buf[t, 0, rows].astype(jnp.float32)
        total += near_buf[t, 1, rows].astype(jnp.float32)
        gate = mod[2, :, pl.ds(pl.multiple_of(y * share, 128), share)]
        y_buf[t, rows] = (rows_buf[t, y, rows].astype(jnp.float32) + gate * total).astype(
            jnp.bfloat16
        )
        shift_copy(t, c).start()

    def arrive(t, c):
        shift_copy(t - 1, c).wait_recv()
        gather_send(t, c)

    def pipeline(stages):
        def step(i, carry):
            for late, stage in enumerate(stages):

                @pl.when(jnp.logical_and(i >= late, i < CHUNKS + late))
                def _():
                    stage(i - late)

            return carry

        lax.fori_loop(0, CHUNKS + len(stages) - 1, step, 0)

    state_in.wait()
    for c in range(CHUNKS):
        gather_send(0, c)
    mod_in.wait()
    stale_in.wait()
    slot = lax.rem(4 * sections - section, 4)
    for place, later in ((0, 1), (patch + text, 2), (2 * patch + text, 3)):
        which = jnp.full((patch, inner), order_ref[lax.rem(slot + later, 4)], jnp.int32)
        picked = [stale[s, text : text + patch].astype(jnp.float32) for s in range(2)]
        for k in range(1, 4):
            source = slice(text + k * patch, text + (k + 1) * patch)
            for s in range(2):
                picked[s] = jnp.where(which == k, stale[s, source].astype(jnp.float32), picked[s])
        k_buf[place : place + patch] = picked[0].astype(jnp.bfloat16)
        for h in range(heads):
            v_buf[place : place + patch, 2 * h * HEAD_DIM : (2 * h + 1) * HEAD_DIM] = picked[1][
                :, h * HEAD_DIM : (h + 1) * HEAD_DIM
            ].astype(jnp.bfloat16)
    k_buf[patch : patch + text] = stale[0, :text]
    for h in range(heads):
        v_buf[patch : patch + text, 2 * h * HEAD_DIM : (2 * h + 1) * HEAD_DIM] = stale[
            1, :text, h * HEAD_DIM : (h + 1) * HEAD_DIM
        ]
        v_buf[:, (2 * h + 1) * HEAD_DIM : 2 * (h + 1) * HEAD_DIM] = jnp.ones(
            (keys + patch, HEAD_DIM), jnp.bfloat16
        )
    wqkv_in.wait()
    wout_in.wait()

    pipeline([functools.partial(gather_pass, 0), functools.partial(project, 0)])
    pipeline(
        [functools.partial(stage, 0) for stage in (attend, combine, finish)]
        + [functools.partial(stage, 1) for stage in (arrive, gather_pass, project)]
    )
    copies = []
    for t in range(TICKS):
        place = slice(fresh_row(t), fresh_row(t) + patch)
        copies.append(
            pltpu.make_async_copy(k_buf.at[place], fresh_ref.at[t, 0], local_sem.at[5 + 4 * t])
        )
        for h in range(heads):
            copies.append(
                pltpu.make_async_copy(
                    v_buf.at[place, 2 * h * HEAD_DIM : (2 * h + 1) * HEAD_DIM],
                    fresh_ref.at[t, 1, :, h * HEAD_DIM : (h + 1) * HEAD_DIM],
                    local_sem.at[6 + 4 * t + h],
                )
            )
    for copy in copies:
        copy.start()
    pipeline([functools.partial(stage, 1) for stage in (attend, combine, finish)])

    for copy in copies:
        copy.wait()

    def drain(c, carry):
        shift_copy(TICKS - 1, c).wait_recv()
        for t in range(TICKS):
            own_copy(t, c, OWN_RIGHT, y, to_right).wait_send()
            own_copy(t, c, OWN_LEFT, y, to_left).wait_send()
            pass_copy(t, c, PASS_RIGHT, left, to_right).wait_send()
            pass_copy(t, c, PASS_LEFT, right, to_left).wait_send()
            far_copy(t, c, FAR_RIGHT, across, to_right).wait_send()
            far_copy(t, c, FAR_LEFT, across, to_left).wait_send()
            near_copy(t, c, PLAIN_RIGHT, right, to_right).wait_send()
            near_copy(t, c, PLAIN_LEFT, left, to_left).wait_send()
            near_copy(t, c, SUM_RIGHT, right, to_right).wait_send()
            near_copy(t, c, SUM_LEFT, left, to_left).wait_send()
            shift_copy(t, c).wait_send()
        return carry

    lax.fori_loop(0, CHUNKS, drain, 0)


def solution(mesh):
    sections = mesh.shape["section"]

    def per_device(state, modulation, w_qkv, w_out, stale_kv, patch_order, text_count):
        patch, share = state.shape[1:]
        width = modulation.shape[2]
        inner = w_out.shape[1]
        keys = stale_kv.shape[2]
        heads = inner // HEAD_DIM
        bf16 = jnp.bfloat16
        anywhere = pl.BlockSpec(memory_space=pl.ANY)
        scalars = pl.BlockSpec(memory_space=pltpu.SMEM)
        flops = TICKS * 2 * patch * inner * (3 * width + 2 * keys + width)
        out, fresh = pl.pallas_call(
            functools.partial(kernel, sections),
            out_shape=(
                jax.ShapeDtypeStruct((patch, share), bf16),
                jax.ShapeDtypeStruct((TICKS, 2, patch, inner), bf16),
            ),
            in_specs=[scalars, scalars] + [anywhere] * 5,
            out_specs=(anywhere, anywhere),
            scratch_shapes=[
                pltpu.VMEM((TICKS, 4, patch, share), bf16),
                pltpu.VMEM((TICKS, 4, patch, share), bf16),
                pltpu.VMEM((TICKS, 2, patch // 2, share), bf16),
                pltpu.VMEM((TICKS, 2, patch, share), bf16),
                pltpu.VMEM((TICKS, patch, share), bf16),
                pltpu.VMEM((3, 1, width), jnp.float32),
                pltpu.VMEM((3, width, inner), bf16),
                pltpu.VMEM((inner, width), bf16),
                pltpu.VMEM((2, keys, inner), bf16),
                pltpu.VMEM((patch, inner), bf16),
                pltpu.VMEM((keys + patch, inner), bf16),
                pltpu.VMEM((keys + patch, 2 * heads * HEAD_DIM), bf16),
                pltpu.SemaphoreType.DMA((16,)),
                pltpu.SemaphoreType.DMA((TICKS, CHUNKS, KINDS)),
                pltpu.SemaphoreType.DMA((TICKS, CHUNKS, KINDS)),
            ],
            compiler_params=pltpu.CompilerParams(
                collective_id=0, has_side_effects=True, vmem_limit_bytes=48 * 2**20
            ),
            cost_estimate=pl.CostEstimate(
                flops=flops, bytes_accessed=14 * 2**20, transcendentals=TICKS * patch * keys * heads
            ),
        )(
            patch_order,
            text_count,
            state[0],
            jnp.transpose(modulation, (1, 0, 2)),
            jnp.transpose(w_qkv[0], (1, 0, 2)),
            w_out[0],
            stale_kv[0],
        )
        return out[None], fresh[None]

    return jax.shard_map(
        per_device,
        mesh=mesh,
        in_specs=(
            P("section", None, "head"),
            P("section", None, None),
            P("section", None, None, "head"),
            P("section", "head", None),
            P("section", None, None, "head"),
            P(),
            P(),
        ),
        out_specs=(P("section", None, "head"), P("section", None, None, None, "head")),
        check_vma=False,
    )
```

```python
import functools

import jax
import jax.numpy as jnp
from jax import lax
from jax.experimental import pallas as pl
from jax.experimental.pallas import tpu as pltpu
from jax.sharding import PartitionSpec as P

MESH = pl.DeviceIdType.MESH
HEAD_DIM = 128
TICKS = 2
EPSILON = 1e-06
SPANS = ((0, 128), (128, 128))

(
    OWN_RIGHT,
    OWN_LEFT,
    PASS_RIGHT,
    PASS_LEFT,
    FAR_RIGHT,
    FAR_LEFT,
    PLAIN_RIGHT,
    PLAIN_LEFT,
    SUM_RIGHT,
    SUM_LEFT,
    SHIFT,
    KINDS,
) = range(12)


def spans_of(patch):
    return [(start * patch // 256, size * patch // 256) for start, size in SPANS]


def kernel(
    sections,
    order_ref,
    count_ref,
    state_ref,
    mod_ref,
    wqkv_ref,
    wout_ref,
    stale_ref,
    out_ref,
    fresh_ref,
    rows_buf,
    terms,
    far_buf,
    near_buf,
    y_buf,
    mod,
    wqkv,
    wout,
    stale,
    h_buf,
    q_buf,
    k_buf,
    v_buf,
    local_sem,
    send_sem,
    recv_sem,
    go_sem,
):
    section = lax.axis_index("section")
    y = lax.axis_index("head")
    ny = 4
    right, left, across = lax.rem(y + 1, ny), lax.rem(y + 3, ny), lax.rem(y + 2, ny)
    behind = lax.rem(section + sections - 1, sections)
    ahead = lax.rem(section + 1, sections)
    to_right, to_left, to_ahead = (section, right), (section, left), (ahead, y)

    patch, share = state_ref.shape
    inner = wout_ref.shape[0]
    heads = inner // HEAD_DIM
    keys = stale_ref.shape[1]
    text = keys - 4 * patch
    width = ny * share
    spans = spans_of(patch)
    chunks = len(spans)

    loads = [
        (state_ref, rows_buf.at[0, y]),
        (stale_ref, stale),
        (mod_ref, mod),
    ]
    for s in range(3):
        loads.append((wqkv_ref.at[s], wqkv.at[:, s * inner : (s + 1) * inner]))
    loads.append((wout_ref, wout))
    loads = [
        pltpu.make_async_copy(source, target, local_sem.at[i])
        for i, (source, target) in enumerate(loads)
    ]
    for load in loads:
        load.start()

    barrier = pltpu.get_barrier_semaphore()
    for target in (to_right, to_left, (behind, y)):
        pl.semaphore_signal(barrier, inc=1, device_id=target, device_id_type=MESH)
    pl.semaphore_wait(barrier, 3)

    def rows_of(c):
        start, size = spans[c]
        return slice(start, start + size)

    def half_of(c, second):
        start, size = spans[c]
        start += second * (size // 2)
        return slice(start, start + size // 2)

    def remote(t, c, kind, source, target, device):
        return pltpu.make_async_remote_copy(
            src_ref=source,
            dst_ref=target,
            send_sem=send_sem.at[t, c, kind],
            recv_sem=recv_sem.at[t, c, kind],
            device_id=device,
            device_id_type=MESH,
        )

    def own_copy(t, c, kind, who, device):
        ref = rows_buf.at[t, who, rows_of(c)]
        return remote(t, c, kind, ref, ref, device)

    def pass_copy(t, c, kind, who, device):
        ref = rows_buf.at[t, who, half_of(c, kind == PASS_LEFT)]
        return remote(t, c, kind, ref, ref, device)

    def far_copy(t, c, kind, who, device):
        rows = half_of(c, kind == FAR_LEFT)
        return remote(t, c, kind, terms.at[t, who, rows], far_buf.at[t, rows], device)

    def near_copy(t, c, kind, who, device):
        side = 0 if kind in (PLAIN_RIGHT, SUM_RIGHT) else 1
        rows = half_of(c, kind in (PLAIN_RIGHT, SUM_LEFT))
        return remote(t, c, kind, terms.at[t, who, rows], near_buf.at[t, side, rows], device)

    def shift_copy(t, c):
        if t + 1 < TICKS:
            target = rows_buf.at[t + 1, y, rows_of(c)]
        else:
            target = out_ref.at[rows_of(c)]
        return remote(t, c, SHIFT, y_buf.at[t, rows_of(c)], target, to_ahead)

    def gather_send(t, c):
        own_copy(t, c, OWN_RIGHT, y, to_right).start()
        own_copy(t, c, OWN_LEFT, y, to_left).start()

    def gather_pass(t, c):
        own_copy(t, c, OWN_RIGHT, left, to_right).wait_recv()
        pass_copy(t, c, PASS_RIGHT, left, to_right).start()
        own_copy(t, c, OWN_LEFT, right, to_left).wait_recv()
        pass_copy(t, c, PASS_LEFT, right, to_left).start()

    def project(t, c):
        pass_copy(t, c, PASS_RIGHT, across, to_right).wait_recv()
        pass_copy(t, c, PASS_LEFT, across, to_left).wait_recv()
        start, size = spans[c]
        rows = rows_of(c)
        centre = mean_of([rows_buf[t, j, rows].astype(jnp.float32) for j in range(ny)])
        squares = []
        for j in range(ny):
            gap = rows_buf[t, j, rows].astype(jnp.float32) - centre
            squares.append(gap * gap)
        factor = lax.rsqrt(mean_of(squares) + EPSILON)
        for j in range(ny):
            columns = slice(j * share, (j + 1) * share)
            gap = rows_buf[t, j, rows].astype(jnp.float32) - centre
            normed = gap * factor * (1.0 + mod[1, :, columns]) + mod[0, :, columns]
            h_buf[rows, columns] = normed.astype(jnp.bfloat16)
        sums = jnp.dot(h_buf[rows], wqkv[...], preferred_element_type=jnp.float32)
        place = slice(fresh_row(t) + start, fresh_row(t) + start + size)
        for h in range(heads):
            columns = slice(h * HEAD_DIM, (h + 1) * HEAD_DIM)
            q_buf[rows, columns] = head_norm(sums[:, columns])
            fresh_key = head_norm(sums[:, inner + h * HEAD_DIM : inner + (h + 1) * HEAD_DIM])
            k_buf[place, columns] = fresh_key
            fresh_ref[t, 0, rows, columns] = fresh_key
            first = 2 * inner + h * HEAD_DIM
            fresh_value = sums[:, first : first + HEAD_DIM].astype(jnp.bfloat16)
            v_buf[place, 2 * h * HEAD_DIM : (2 * h + 1) * HEAD_DIM] = fresh_value
            fresh_ref[t, 1, rows, columns] = fresh_value

    def mean_of(parts):
        folded = None
        for part in parts:
            for k in range(share // HEAD_DIM):
                piece = part[:, k * HEAD_DIM : (k + 1) * HEAD_DIM]
                folded = piece if folded is None else folded + piece
        return jnp.sum(folded, axis=-1, keepdims=True) * (1.0 / width)

    def head_norm(value):
        square = jnp.mean(value * value, axis=-1, keepdims=True)
        return (value * lax.rsqrt(square + EPSILON)).astype(jnp.bfloat16)

    def fresh_row(t):
        return text + 3 * patch + t * patch

    def attend(t, c):
        size = spans[c][1]
        window = slice(t * patch, t * patch + keys)
        text_at = patch if t == 0 else 0
        position = lax.broadcasted_iota(jnp.int32, (size, text), 1)
        alive = position < count_ref[0]
        mixed = []
        for h in range(heads):
            columns = slice(h * HEAD_DIM, (h + 1) * HEAD_DIM)
            scores = lax.dot_general(
                q_buf[rows_of(c), columns],
                k_buf[window, columns],
                (((1,), (1,)), ((), ())),
                preferred_element_type=jnp.float32,
            )
            weights = jnp.exp(scores * HEAD_DIM ** (-0.5))
            pieces = [jnp.where(alive, weights[:, text_at : text_at + text], 0.0)]
            if text_at:
                pieces.insert(0, weights[:, :text_at])
            pieces.append(weights[:, text_at + text :])
            weights = jnp.concatenate(pieces, axis=1).astype(jnp.bfloat16)
            both = jnp.dot(
                weights,
                v_buf[window, 2 * h * HEAD_DIM : 2 * (h + 1) * HEAD_DIM],
                preferred_element_type=jnp.float32,
            )
            mixed.append((both[:, :HEAD_DIM] / both[:, HEAD_DIM:]).astype(jnp.bfloat16))
        mixed = jnp.concatenate(mixed, axis=1)
        for j in range(ny):
            columns = slice(j * share, (j + 1) * share)
            terms[t, j, rows_of(c)] = jnp.dot(
                mixed, wout[:, columns], preferred_element_type=jnp.float32
            ).astype(jnp.bfloat16)
        far_copy(t, c, FAR_RIGHT, across, to_right).start()
        far_copy(t, c, FAR_LEFT, across, to_left).start()

    def plain(t, c):
        near_copy(t, c, PLAIN_RIGHT, right, to_right).start()
        near_copy(t, c, PLAIN_LEFT, left, to_left).start()

    def combine(t, c):
        for far, near, who, device in (
            (FAR_RIGHT, SUM_RIGHT, right, to_right),
            (FAR_LEFT, SUM_LEFT, left, to_left),
        ):
            far_copy(t, c, far, who, device).wait_recv()
            rows = half_of(c, far == FAR_LEFT)
            terms[t, who, rows] = (
                terms[t, who, rows].astype(jnp.float32) + far_buf[t, rows].astype(jnp.float32)
            ).astype(jnp.bfloat16)
            near_copy(t, c, near, who, device).start()

    def finish(t, c):
        for kind in (PLAIN_RIGHT, PLAIN_LEFT, SUM_RIGHT, SUM_LEFT):
            device = to_right if kind in (PLAIN_RIGHT, SUM_RIGHT) else to_left
            near_copy(t, c, kind, y, device).wait_recv()
        rows = rows_of(c)
        total = terms[t, y, rows].astype(jnp.float32)
        total += near_buf[t, 0, rows].astype(jnp.float32)
        total += near_buf[t, 1, rows].astype(jnp.float32)
        gate = mod[2, :, pl.ds(pl.multiple_of(y * share, 128), share)]
        y_buf[t, rows] = (rows_buf[t, y, rows].astype(jnp.float32) + gate * total).astype(
            jnp.bfloat16
        )
        shift_copy(t, c).start()

    def arrive(t, c):
        shift_copy(t - 1, c).wait_recv()
        gather_send(t, c)

    first_core = lax.rem(section, 2) == 0
    loads[0].wait()

    @pl.when(first_core)
    def _():
        for c in range(chunks):
            gather_send(0, c)

    for load in loads[1:2]:
        load.wait()
    slot = lax.rem(4 * sections - section, 4)
    for place, later in ((0, 1), (patch + text, 2), (2 * patch + text, 3)):
        which = jnp.full((patch, inner), order_ref[lax.rem(slot + later, 4)], jnp.int32)
        picked = [stale[s, text : text + patch].astype(jnp.float32) for s in range(2)]
        for k in range(1, 4):
            source = slice(text + k * patch, text + (k + 1) * patch)
            for s in range(2):
                picked[s] = jnp.where(which == k, stale[s, source].astype(jnp.float32), picked[s])
        k_buf[place : place + patch] = picked[0].astype(jnp.bfloat16)
        for h in range(heads):
            v_buf[place : place + patch, 2 * h * HEAD_DIM : (2 * h + 1) * HEAD_DIM] = picked[1][
                :, h * HEAD_DIM : (h + 1) * HEAD_DIM
            ].astype(jnp.bfloat16)
    k_buf[patch : patch + text] = stale[0, :text]
    for h in range(heads):
        v_buf[patch : patch + text, 2 * h * HEAD_DIM : (2 * h + 1) * HEAD_DIM] = stale[
            1, :text, h * HEAD_DIM : (h + 1) * HEAD_DIM
        ]
        v_buf[:, (2 * h + 1) * HEAD_DIM : 2 * (h + 1) * HEAD_DIM] = jnp.ones(
            (keys + patch, HEAD_DIM), jnp.bfloat16
        )

    @pl.when(jnp.logical_not(first_core))
    def _():
        pl.semaphore_wait(go_sem, 1)
        for c in range(chunks):
            gather_send(0, c)

    for t in range(TICKS):
        if t:
            for c in range(chunks):
                arrive(t, c)
        for c in range(chunks):
            gather_pass(t, c)
            if t == 0 and c == 0:

                @pl.when(first_core)
                def _():
                    pl.semaphore_signal(go_sem, inc=1, device_id=to_ahead, device_id_type=MESH)

        if t == 0:
            for load in loads[2:]:
                load.wait()
        for stage in (project, attend, plain, combine, finish):
            for c in range(chunks):
                stage(t, c)

    for c in range(chunks):
        shift_copy(TICKS - 1, c).wait_recv()
        for t in range(TICKS):
            own_copy(t, c, OWN_RIGHT, y, to_right).wait_send()
            own_copy(t, c, OWN_LEFT, y, to_left).wait_send()
            pass_copy(t, c, PASS_RIGHT, left, to_right).wait_send()
            pass_copy(t, c, PASS_LEFT, right, to_left).wait_send()
            far_copy(t, c, FAR_RIGHT, across, to_right).wait_send()
            far_copy(t, c, FAR_LEFT, across, to_left).wait_send()
            near_copy(t, c, PLAIN_RIGHT, right, to_right).wait_send()
            near_copy(t, c, PLAIN_LEFT, left, to_left).wait_send()
            near_copy(t, c, SUM_RIGHT, right, to_right).wait_send()
            near_copy(t, c, SUM_LEFT, left, to_left).wait_send()
            shift_copy(t, c).wait_send()


def solution(mesh):
    sections = mesh.shape["section"]

    def per_device(state, modulation, w_qkv, w_out, stale_kv, patch_order, text_count):
        patch, share = state.shape[1:]
        width = modulation.shape[2]
        inner = w_out.shape[1]
        keys = stale_kv.shape[2]
        heads = inner // HEAD_DIM
        bf16 = jnp.bfloat16
        anywhere = pl.BlockSpec(memory_space=pl.ANY)
        chunks = len(spans_of(patch))
        flops = TICKS * 2 * patch * inner * (3 * width + 2 * keys + width)
        out, fresh = pl.pallas_call(
            functools.partial(kernel, sections),
            out_shape=(
                pltpu.VMEM((patch, share), bf16),
                pltpu.VMEM((TICKS, 2, patch, inner), bf16),
            ),
            in_specs=[pl.BlockSpec(memory_space=pltpu.SMEM)] * 2 + [anywhere] * 5,
            out_specs=(pl.BlockSpec(memory_space=pltpu.VMEM),) * 2,
            scratch_shapes=[
                pltpu.VMEM((TICKS, 4, patch, share), bf16),
                pltpu.VMEM((TICKS, 4, patch, share), bf16),
                pltpu.VMEM((TICKS, patch, share), bf16),
                pltpu.VMEM((TICKS, 2, patch, share), bf16),
                pltpu.VMEM((TICKS, patch, share), bf16),
                pltpu.VMEM((3, 1, width), jnp.float32),
                pltpu.VMEM((width, 3 * inner), bf16),
                pltpu.VMEM((inner, width), bf16),
                pltpu.VMEM((2, keys, inner), bf16),
                pltpu.VMEM((patch, width), bf16),
                pltpu.VMEM((patch, inner), bf16),
                pltpu.VMEM((keys + patch, inner), bf16),
                pltpu.VMEM((keys + patch, 2 * heads * HEAD_DIM), bf16),
                pltpu.SemaphoreType.DMA((16,)),
                pltpu.SemaphoreType.DMA((TICKS, chunks, KINDS)),
                pltpu.SemaphoreType.DMA((TICKS, chunks, KINDS)),
                pltpu.SemaphoreType.REGULAR,
            ],
            compiler_params=pltpu.CompilerParams(
                collective_id=0, has_side_effects=True, vmem_limit_bytes=48 * 2**20
            ),
            cost_estimate=pl.CostEstimate(
                flops=flops, bytes_accessed=14 * 2**20, transcendentals=TICKS * patch * keys * heads
            ),
        )(
            pltpu.with_memory_space_constraint(patch_order, pltpu.HBM),
            text_count,
            *(
                pltpu.with_memory_space_constraint(value, pltpu.HBM)
                for value in (
                    state[0],
                    jnp.transpose(modulation, (1, 0, 2)),
                    jnp.transpose(w_qkv[0], (1, 0, 2)),
                    w_out[0],
                    stale_kv[0],
                )
            ),
        )
        return out[None], fresh[None]

    return jax.shard_map(
        per_device,
        mesh=mesh,
        in_specs=(
            P("section", None, "head"),
            P("section", None, None),
            P("section", None, None, "head"),
            P("section", "head", None),
            P("section", None, None, "head"),
            P(),
            P(),
        ),
        out_specs=(P("section", None, "head"), P("section", None, None, None, "head")),
        check_vma=False,
    )
```

```python
import functools

import jax
import jax.numpy as jnp
from jax import lax
from jax.experimental import pallas as pl
from jax.experimental.pallas import tpu as pltpu
from jax.sharding import PartitionSpec as P

MESH = pl.DeviceIdType.MESH
HEAD_DIM = 128
TICKS = 2
EPSILON = 1e-06
SPANS = ((0, 64), (64, 64), (128, 64), (192, 64))
GROUPS = ((0, 1), (2, 3))


(
    OWN_RIGHT,
    OWN_LEFT,
    PASS_RIGHT,
    PASS_LEFT,
    FAR_RIGHT,
    FAR_LEFT,
    PLAIN_RIGHT,
    PLAIN_LEFT,
    SUM_RIGHT,
    SUM_LEFT,
    SHIFT,
    KINDS,
) = range(12)


def spans_of(patch):
    return [(start * patch // 256, size * patch // 256) for start, size in SPANS]


def kernel(
    sections,
    order_ref,
    count_ref,
    state_ref,
    mod_ref,
    wqkv_ref,
    wout_ref,
    stale_ref,
    out_ref,
    fresh_ref,
    rows_buf,
    terms,
    far_buf,
    near_buf,
    y_buf,
    mod,
    wqkv,
    wout,
    stale,
    h_buf,
    early,
    q_buf,
    k_buf,
    v_buf,
    local_sem,
    send_sem,
    recv_sem,
    go_sem,
):
    section = lax.axis_index("section")
    y = lax.axis_index("head")
    ny = 4
    right, left, across = lax.rem(y + 1, ny), lax.rem(y + 3, ny), lax.rem(y + 2, ny)
    behind = lax.rem(section + sections - 1, sections)
    ahead = lax.rem(section + 1, sections)
    to_right, to_left, to_ahead = (section, right), (section, left), (ahead, y)

    patch, share = state_ref.shape
    inner = wout_ref.shape[0]
    heads = inner // HEAD_DIM
    keys = stale_ref.shape[1]
    text = keys - 4 * patch
    width = ny * share
    spans = spans_of(patch)
    chunks = len(spans)

    loads = [
        (state_ref, rows_buf.at[0, y]),
        (stale_ref, stale),
        (mod_ref, mod),
    ]
    for s in range(3):
        loads.append((wqkv_ref.at[s], wqkv.at[:, s * inner : (s + 1) * inner]))
    loads.append((wout_ref, wout))
    loads = [
        pltpu.make_async_copy(source, target, local_sem.at[i])
        for i, (source, target) in enumerate(loads)
    ]
    for load in loads:
        load.start()

    barrier = pltpu.get_barrier_semaphore()
    for target in (to_right, to_left, (behind, y)):
        pl.semaphore_signal(barrier, inc=1, device_id=target, device_id_type=MESH)
    pl.semaphore_wait(barrier, 3)

    def rows_of(c):
        start, size = spans[c]
        return slice(start, start + size)

    def half_of(c, second):
        start, size = spans[c]
        start += second * (size // 2)
        return slice(start, start + size // 2)

    def remote(t, c, kind, source, target, device):
        return pltpu.make_async_remote_copy(
            src_ref=source,
            dst_ref=target,
            send_sem=send_sem.at[t, c, kind],
            recv_sem=recv_sem.at[t, c, kind],
            device_id=device,
            device_id_type=MESH,
        )

    def own_copy(t, c, kind, who, device):
        ref = rows_buf.at[t, who, rows_of(c)]
        return remote(t, c, kind, ref, ref, device)

    def pass_copy(t, c, kind, who, device):
        ref = rows_buf.at[t, who, half_of(c, kind == PASS_LEFT)]
        return remote(t, c, kind, ref, ref, device)

    def far_copy(t, c, kind, who, device):
        rows = half_of(c, kind == FAR_LEFT)
        return remote(t, c, kind, terms.at[t, who, rows], far_buf.at[t, rows], device)

    def near_copy(t, c, kind, who, device):
        side = 0 if kind in (PLAIN_RIGHT, SUM_RIGHT) else 1
        rows = half_of(c, kind in (PLAIN_RIGHT, SUM_LEFT))
        return remote(t, c, kind, terms.at[t, who, rows], near_buf.at[t, side, rows], device)

    def shift_copy(t, c):
        if t + 1 < TICKS:
            target = rows_buf.at[t + 1, y, rows_of(c)]
        else:
            target = out_ref.at[rows_of(c)]
        return remote(t, c, SHIFT, y_buf.at[t, rows_of(c)], target, to_ahead)

    def gather_send(t, c):
        own_copy(t, c, OWN_RIGHT, y, to_right).start()
        own_copy(t, c, OWN_LEFT, y, to_left).start()

    def gather_pass(t, c):
        own_copy(t, c, OWN_RIGHT, left, to_right).wait_recv()
        pass_copy(t, c, PASS_RIGHT, left, to_right).start()
        own_copy(t, c, OWN_LEFT, right, to_left).wait_recv()
        pass_copy(t, c, PASS_LEFT, right, to_left).start()

    def group_rows(g):
        start = spans[GROUPS[g][0]][0]
        return start, sum(spans[c][1] for c in GROUPS[g])

    def project(t, g):
        for c in GROUPS[g]:
            pass_copy(t, c, PASS_RIGHT, across, to_right).wait_recv()
            pass_copy(t, c, PASS_LEFT, across, to_left).wait_recv()
        start, size = group_rows(g)
        rows = slice(start, start + size)
        centre = mean_of([rows_buf[t, j, rows].astype(jnp.float32) for j in range(ny)])
        squares = []
        for j in range(ny):
            gap = rows_buf[t, j, rows].astype(jnp.float32) - centre
            squares.append(gap * gap)
        factor = lax.rsqrt(mean_of(squares) + EPSILON)
        for j in range(ny):
            columns = slice(j * share, (j + 1) * share)
            gap = rows_buf[t, j, rows].astype(jnp.float32) - centre
            normed = gap * factor * (1.0 + mod[1, :, columns]) + mod[0, :, columns]
            h_buf[rows, columns] = normed.astype(jnp.bfloat16)
        sums = jnp.dot(h_buf[rows], wqkv[...], preferred_element_type=jnp.float32)
        place = slice(fresh_row(t) + start, fresh_row(t) + start + size)
        for h in range(heads):
            columns = slice(h * HEAD_DIM, (h + 1) * HEAD_DIM)
            q_buf[rows, columns] = head_norm(sums[:, columns])
            fresh_key = head_norm(sums[:, inner + h * HEAD_DIM : inner + (h + 1) * HEAD_DIM])
            k_buf[place, columns] = fresh_key
            fresh_ref[t, 0, rows, columns] = fresh_key
            first = 2 * inner + h * HEAD_DIM
            fresh_value = sums[:, first : first + HEAD_DIM].astype(jnp.bfloat16)
            v_buf[place, 2 * h * HEAD_DIM : (2 * h + 1) * HEAD_DIM] = fresh_value
            fresh_ref[t, 1, rows, columns] = fresh_value

    def mean_of(parts):
        folded = None
        for part in parts:
            for k in range(share // HEAD_DIM):
                piece = part[:, k * HEAD_DIM : (k + 1) * HEAD_DIM]
                folded = piece if folded is None else folded + piece
        return jnp.sum(folded, axis=-1, keepdims=True) * (1.0 / width)

    def head_norm(value):
        square = jnp.mean(value * value, axis=-1, keepdims=True)
        return (value * lax.rsqrt(square + EPSILON)).astype(jnp.bfloat16)

    def fresh_row(t):
        return text + 3 * patch + t * patch

    def attention(t, g, h, first, last):
        start, size = group_rows(g)
        columns = slice(h * HEAD_DIM, (h + 1) * HEAD_DIM)
        window = slice(t * patch + first, t * patch + last)
        scores = lax.dot_general(
            q_buf[start : start + size, columns],
            k_buf[window, columns],
            (((1,), (1,)), ((), ())),
            preferred_element_type=jnp.float32,
        )
        weights = jnp.exp(scores * HEAD_DIM ** (-0.5))
        text_at = patch if t == 0 else 0
        if first <= text_at < last:
            position = lax.broadcasted_iota(jnp.int32, (size, text), 1)
            alive = position < count_ref[0]
            pieces = [jnp.where(alive, weights[:, text_at : text_at + text], 0.0)]
            if text_at:
                pieces.insert(0, weights[:, :text_at])
            pieces.append(weights[:, text_at + text :])
            weights = jnp.concatenate(pieces, axis=1)
        return jnp.dot(
            weights.astype(jnp.bfloat16),
            v_buf[window, 2 * h * HEAD_DIM : 2 * (h + 1) * HEAD_DIM],
            preferred_element_type=jnp.float32,
        )

    known = keys - group_rows(len(GROUPS) - 1)[1]

    def attend_early(t, g):
        start, size = group_rows(g)
        for h in range(heads):
            early[h, start : start + size] = attention(t, g, h, 0, known)

    def attend(t, g):
        start, size = group_rows(g)
        rows = slice(start, start + size)
        mixed = []
        for h in range(heads):
            if g < len(GROUPS) - 1:
                both = early[h, rows] + attention(t, g, h, known, keys)
            else:
                both = attention(t, g, h, 0, keys)
            mixed.append((both[:, :HEAD_DIM] / both[:, HEAD_DIM:]).astype(jnp.bfloat16))
        mixed = jnp.concatenate(mixed, axis=1)
        for j in range(ny):
            columns = slice(j * share, (j + 1) * share)
            terms[t, j, rows] = jnp.dot(
                mixed, wout[:, columns], preferred_element_type=jnp.float32
            ).astype(jnp.bfloat16)
        for c in GROUPS[g]:
            far_copy(t, c, FAR_RIGHT, across, to_right).start()
            far_copy(t, c, FAR_LEFT, across, to_left).start()

    def plain(t, c):
        near_copy(t, c, PLAIN_RIGHT, right, to_right).start()
        near_copy(t, c, PLAIN_LEFT, left, to_left).start()

    def combine(t, c):
        for far, near, who, device in (
            (FAR_RIGHT, SUM_RIGHT, right, to_right),
            (FAR_LEFT, SUM_LEFT, left, to_left),
        ):
            far_copy(t, c, far, who, device).wait_recv()
            rows = half_of(c, far == FAR_LEFT)
            terms[t, who, rows] = (
                terms[t, who, rows].astype(jnp.float32) + far_buf[t, rows].astype(jnp.float32)
            ).astype(jnp.bfloat16)
            near_copy(t, c, near, who, device).start()

    def finish(t, c):
        for kind in (PLAIN_RIGHT, PLAIN_LEFT, SUM_RIGHT, SUM_LEFT):
            device = to_right if kind in (PLAIN_RIGHT, SUM_RIGHT) else to_left
            near_copy(t, c, kind, y, device).wait_recv()
        rows = rows_of(c)
        total = terms[t, y, rows].astype(jnp.float32)
        total += near_buf[t, 0, rows].astype(jnp.float32)
        total += near_buf[t, 1, rows].astype(jnp.float32)
        gate = mod[2, :, pl.ds(pl.multiple_of(y * share, 128), share)]
        y_buf[t, rows] = (rows_buf[t, y, rows].astype(jnp.float32) + gate * total).astype(
            jnp.bfloat16
        )
        shift_copy(t, c).start()

    def arrive(t, c):
        shift_copy(t - 1, c).wait_recv()
        gather_send(t, c)

    first_core = lax.rem(section, 2) == 0
    loads[0].wait()

    @pl.when(first_core)
    def _():
        for c in range(chunks):
            gather_send(0, c)

    for load in loads[1:2]:
        load.wait()
    slot = lax.rem(4 * sections - section, 4)
    for place, later in ((0, 1), (patch + text, 2), (2 * patch + text, 3)):
        which = jnp.full((patch, inner), order_ref[lax.rem(slot + later, 4)], jnp.int32)
        picked = [stale[s, text : text + patch].astype(jnp.float32) for s in range(2)]
        for k in range(1, 4):
            source = slice(text + k * patch, text + (k + 1) * patch)
            for s in range(2):
                picked[s] = jnp.where(which == k, stale[s, source].astype(jnp.float32), picked[s])
        k_buf[place : place + patch] = picked[0].astype(jnp.bfloat16)
        for h in range(heads):
            v_buf[place : place + patch, 2 * h * HEAD_DIM : (2 * h + 1) * HEAD_DIM] = picked[1][
                :, h * HEAD_DIM : (h + 1) * HEAD_DIM
            ].astype(jnp.bfloat16)
    k_buf[patch : patch + text] = stale[0, :text]
    for h in range(heads):
        v_buf[patch : patch + text, 2 * h * HEAD_DIM : (2 * h + 1) * HEAD_DIM] = stale[
            1, :text, h * HEAD_DIM : (h + 1) * HEAD_DIM
        ]
        v_buf[:, (2 * h + 1) * HEAD_DIM : 2 * (h + 1) * HEAD_DIM] = jnp.ones(
            (keys + patch, HEAD_DIM), jnp.bfloat16
        )

    @pl.when(jnp.logical_not(first_core))
    def _():
        pl.semaphore_wait(go_sem, 1)
        for c in range(chunks):
            gather_send(0, c)

    everything = range(chunks)
    for t in range(TICKS):
        for c in everything:
            gather_pass(t, c)
            if t == 0 and c == 0:

                @pl.when(first_core)
                def _():
                    pl.semaphore_signal(go_sem, inc=1, device_id=to_ahead, device_id_type=MESH)

        if t == 1:

            @pl.when(lax.rem(section, sections // 4) == 0)
            def _():
                pl.semaphore_signal(go_sem, inc=1, device_id=to_ahead, device_id_type=MESH)

        if t == 0:
            for load in loads[2:]:
                load.wait()
        for g in range(len(GROUPS)):
            project(t, g)
            if g < len(GROUPS) - 1:
                attend_early(t, g)
        if t == 1:

            @pl.when(lax.rem(section, sections // 4) == 1)
            def _():
                pl.semaphore_wait(go_sem, 1)

        for g in range(len(GROUPS)):
            attend(t, g)
        for c in everything:
            plain(t, c)
        for c in everything:
            combine(t, c)
        if t + 1 < TICKS:

            @pl.when(jnp.logical_not(first_core))
            def _():
                for c in everything:
                    arrive(t + 1, c)

        for c in everything:
            finish(t, c)
        if t + 1 < TICKS:

            @pl.when(first_core)
            def _():
                for c in everything:
                    arrive(t + 1, c)

    for c in range(chunks):
        shift_copy(TICKS - 1, c).wait_recv()
        for t in range(TICKS):
            own_copy(t, c, OWN_RIGHT, y, to_right).wait_send()
            own_copy(t, c, OWN_LEFT, y, to_left).wait_send()
            pass_copy(t, c, PASS_RIGHT, left, to_right).wait_send()
            pass_copy(t, c, PASS_LEFT, right, to_left).wait_send()
            far_copy(t, c, FAR_RIGHT, across, to_right).wait_send()
            far_copy(t, c, FAR_LEFT, across, to_left).wait_send()
            near_copy(t, c, PLAIN_RIGHT, right, to_right).wait_send()
            near_copy(t, c, PLAIN_LEFT, left, to_left).wait_send()
            near_copy(t, c, SUM_RIGHT, right, to_right).wait_send()
            near_copy(t, c, SUM_LEFT, left, to_left).wait_send()
            shift_copy(t, c).wait_send()


def solution(mesh):
    sections = mesh.shape["section"]

    def per_device(state, modulation, w_qkv, w_out, stale_kv, patch_order, text_count):
        patch, share = state.shape[1:]
        width = modulation.shape[2]
        inner = w_out.shape[1]
        keys = stale_kv.shape[2]
        heads = inner // HEAD_DIM
        bf16 = jnp.bfloat16
        anywhere = pl.BlockSpec(memory_space=pl.ANY)
        chunks = len(spans_of(patch))
        flops = TICKS * 2 * patch * inner * (3 * width + 2 * keys + width)
        out, fresh = pl.pallas_call(
            functools.partial(kernel, sections),
            out_shape=(
                pltpu.VMEM((patch, share), bf16),
                pltpu.VMEM((TICKS, 2, patch, inner), bf16),
            ),
            in_specs=[pl.BlockSpec(memory_space=pltpu.SMEM)] * 2 + [anywhere] * 5,
            out_specs=(pl.BlockSpec(memory_space=pltpu.VMEM),) * 2,
            scratch_shapes=[
                pltpu.VMEM((TICKS, 4, patch, share), bf16),
                pltpu.VMEM((TICKS, 4, patch, share), bf16),
                pltpu.VMEM((TICKS, patch, share), bf16),
                pltpu.VMEM((TICKS, 2, patch, share), bf16),
                pltpu.VMEM((TICKS, patch, share), bf16),
                pltpu.VMEM((3, 1, width), jnp.float32),
                pltpu.VMEM((width, 3 * inner), bf16),
                pltpu.VMEM((inner, width), bf16),
                pltpu.VMEM((2, keys, inner), bf16),
                pltpu.VMEM((patch, width), bf16),
                pltpu.VMEM((heads, patch, 2 * HEAD_DIM), jnp.float32),
                pltpu.VMEM((patch, inner), bf16),
                pltpu.VMEM((keys + patch, inner), bf16),
                pltpu.VMEM((keys + patch, 2 * heads * HEAD_DIM), bf16),
                pltpu.SemaphoreType.DMA((16,)),
                pltpu.SemaphoreType.DMA((TICKS, chunks, KINDS)),
                pltpu.SemaphoreType.DMA((TICKS, chunks, KINDS)),
                pltpu.SemaphoreType.REGULAR,
            ],
            compiler_params=pltpu.CompilerParams(
                collective_id=0, has_side_effects=True, vmem_limit_bytes=48 * 2**20
            ),
            cost_estimate=pl.CostEstimate(
                flops=flops, bytes_accessed=14 * 2**20, transcendentals=TICKS * patch * keys * heads
            ),
        )(
            pltpu.with_memory_space_constraint(patch_order, pltpu.HBM),
            text_count,
            *(
                pltpu.with_memory_space_constraint(value, pltpu.HBM)
                for value in (
                    state[0],
                    jnp.transpose(modulation, (1, 0, 2)),
                    jnp.transpose(w_qkv[0], (1, 0, 2)),
                    w_out[0],
                    stale_kv[0],
                )
            ),
        )
        return out[None], fresh[None]

    return jax.shard_map(
        per_device,
        mesh=mesh,
        in_specs=(
            P("section", None, "head"),
            P("section", None, None),
            P("section", None, None, "head"),
            P("section", "head", None),
            P("section", None, None, "head"),
            P(),
            P(),
        ),
        out_specs=(P("section", None, "head"), P("section", None, None, None, "head")),
        check_vma=False,
    )
```

```python
import functools

import jax
import jax.numpy as jnp
from jax import lax
from jax.experimental import pallas as pl
from jax.experimental.pallas import tpu as pltpu
from jax.sharding import PartitionSpec as P

MESH = pl.DeviceIdType.MESH
HEAD_DIM = 128
TICKS = 2
EPSILON = 1e-06
SPANS = ((0, 64), (64, 64), (128, 64), (192, 64))
GROUPS = ((0, 1), (2, 3))


(
    OWN_RIGHT,
    OWN_LEFT,
    PASS_RIGHT,
    PASS_LEFT,
    FAR_RIGHT,
    FAR_LEFT,
    PLAIN_RIGHT,
    PLAIN_LEFT,
    SUM_RIGHT,
    SUM_LEFT,
    SHIFT,
    KINDS,
) = range(12)


def spans_of(patch):
    return [(start * patch // 256, size * patch // 256) for start, size in SPANS]


def kernel(
    sections,
    order_ref,
    count_ref,
    state_ref,
    mod_ref,
    wqkv_ref,
    wout_ref,
    stale_ref,
    out_ref,
    fresh_ref,
    rows_buf,
    terms,
    far_buf,
    near_buf,
    y_buf,
    mod,
    wqkv,
    wout,
    stale,
    h_buf,
    early,
    q_buf,
    k_buf,
    v_buf,
    local_sem,
    send_sem,
    recv_sem,
    go_sem,
):
    section = lax.axis_index("section")
    y = lax.axis_index("head")
    ny = 4
    right, left, across = lax.rem(y + 1, ny), lax.rem(y + 3, ny), lax.rem(y + 2, ny)
    behind = lax.rem(section + sections - 1, sections)
    ahead = lax.rem(section + 1, sections)
    to_right, to_left, to_ahead = (section, right), (section, left), (ahead, y)

    patch, share = state_ref.shape
    inner = wout_ref.shape[0]
    heads = inner // HEAD_DIM
    keys = stale_ref.shape[1]
    text = keys - 4 * patch
    width = ny * share
    spans = spans_of(patch)
    chunks = len(spans)

    loads = [
        (state_ref, rows_buf.at[0, y]),
        (stale_ref, stale),
        (mod_ref, mod),
    ]
    for s in range(3):
        loads.append((wqkv_ref.at[s], wqkv.at[:, s * inner : (s + 1) * inner]))
    loads.append((wout_ref, wout))
    loads = [
        pltpu.make_async_copy(source, target, local_sem.at[i])
        for i, (source, target) in enumerate(loads)
    ]
    for load in loads:
        load.start()

    barrier = pltpu.get_barrier_semaphore()
    for target in (to_right, to_left, (behind, y)):
        pl.semaphore_signal(barrier, inc=1, device_id=target, device_id_type=MESH)
    pl.semaphore_wait(barrier, 3)

    def rows_of(c):
        start, size = spans[c]
        return slice(start, start + size)

    def half_of(c, second):
        start, size = spans[c]
        start += second * (size // 2)
        return slice(start, start + size // 2)

    def remote(t, c, kind, source, target, device):
        return pltpu.make_async_remote_copy(
            src_ref=source,
            dst_ref=target,
            send_sem=send_sem.at[t, c, kind],
            recv_sem=recv_sem.at[t, c, kind],
            device_id=device,
            device_id_type=MESH,
        )

    def own_copy(t, c, kind, who, device):
        ref = rows_buf.at[t, who, rows_of(c)]
        return remote(t, c, kind, ref, ref, device)

    def pass_copy(t, c, kind, who, device):
        ref = rows_buf.at[t, who, half_of(c, kind == PASS_LEFT)]
        return remote(t, c, kind, ref, ref, device)

    def far_copy(t, c, kind, who, device):
        rows = half_of(c, kind == FAR_LEFT)
        return remote(t, c, kind, terms.at[t, who, rows], far_buf.at[t, rows], device)

    def near_copy(t, c, kind, who, device):
        side = 0 if kind in (PLAIN_RIGHT, SUM_RIGHT) else 1
        rows = half_of(c, kind in (PLAIN_RIGHT, SUM_LEFT))
        return remote(t, c, kind, terms.at[t, who, rows], near_buf.at[t, side, rows], device)

    def shift_copy(t, c):
        if t + 1 < TICKS:
            target = rows_buf.at[t + 1, y, rows_of(c)]
        else:
            target = out_ref.at[rows_of(c)]
        return remote(t, c, SHIFT, y_buf.at[t, rows_of(c)], target, to_ahead)

    def gather_send(t, c):
        own_copy(t, c, OWN_RIGHT, y, to_right).start()
        own_copy(t, c, OWN_LEFT, y, to_left).start()

    def gather_pass(t, c):
        own_copy(t, c, OWN_RIGHT, left, to_right).wait_recv()
        pass_copy(t, c, PASS_RIGHT, left, to_right).start()
        own_copy(t, c, OWN_LEFT, right, to_left).wait_recv()
        pass_copy(t, c, PASS_LEFT, right, to_left).start()

    def group_rows(g):
        start = spans[GROUPS[g][0]][0]
        return start, sum(spans[c][1] for c in GROUPS[g])

    def project(t, g):
        for c in GROUPS[g]:
            pass_copy(t, c, PASS_RIGHT, across, to_right).wait_recv()
            pass_copy(t, c, PASS_LEFT, across, to_left).wait_recv()
        start, size = group_rows(g)
        rows = slice(start, start + size)
        for first in range(start, start + size, 16):
            few = slice(first, first + 16)
            parts = [rows_buf[t, j, few].astype(jnp.float32) for j in range(ny)]
            centre = mean_of(parts)
            parts = [part - centre for part in parts]
            factor = lax.rsqrt(mean_of([part * part for part in parts]) + EPSILON)
            for j in range(ny):
                columns = slice(j * share, (j + 1) * share)
                normed = parts[j] * factor * (1.0 + mod[1, :, columns]) + mod[0, :, columns]
                h_buf[few, columns] = normed.astype(jnp.bfloat16)
        sums = jnp.dot(h_buf[rows], wqkv[...], preferred_element_type=jnp.float32)
        place = slice(fresh_row(t) + start, fresh_row(t) + start + size)
        for h in range(heads):
            columns = slice(h * HEAD_DIM, (h + 1) * HEAD_DIM)
            q_buf[rows, columns] = head_norm(sums[:, columns])
            fresh_key = head_norm(sums[:, inner + h * HEAD_DIM : inner + (h + 1) * HEAD_DIM])
            k_buf[place, columns] = fresh_key
            fresh_ref[t, 0, rows, columns] = fresh_key
            first = 2 * inner + h * HEAD_DIM
            fresh_value = sums[:, first : first + HEAD_DIM].astype(jnp.bfloat16)
            v_buf[place, 2 * h * HEAD_DIM : (2 * h + 1) * HEAD_DIM] = fresh_value
            fresh_ref[t, 1, rows, columns] = fresh_value

    def mean_of(parts):
        folded = None
        for part in parts:
            for k in range(share // HEAD_DIM):
                piece = part[:, k * HEAD_DIM : (k + 1) * HEAD_DIM]
                folded = piece if folded is None else folded + piece
        return jnp.sum(folded, axis=-1, keepdims=True) * (1.0 / width)

    def head_norm(value):
        square = jnp.mean(value * value, axis=-1, keepdims=True)
        return (value * lax.rsqrt(square + EPSILON)).astype(jnp.bfloat16)

    def fresh_row(t):
        return text + 3 * patch + t * patch

    def attention(t, g, h, first, last):
        start, size = group_rows(g)
        columns = slice(h * HEAD_DIM, (h + 1) * HEAD_DIM)
        window = slice(t * patch + first, t * patch + last)
        scores = lax.dot_general(
            q_buf[start : start + size, columns],
            k_buf[window, columns],
            (((1,), (1,)), ((), ())),
            preferred_element_type=jnp.float32,
        )
        weights = jnp.exp(scores * HEAD_DIM ** (-0.5))
        text_at = patch if t == 0 else 0
        if first <= text_at < last:
            position = lax.broadcasted_iota(jnp.int32, (size, text), 1)
            alive = position < count_ref[0]
            pieces = [jnp.where(alive, weights[:, text_at : text_at + text], 0.0)]
            if text_at:
                pieces.insert(0, weights[:, :text_at])
            pieces.append(weights[:, text_at + text :])
            weights = jnp.concatenate(pieces, axis=1)
        return jnp.dot(
            weights.astype(jnp.bfloat16),
            v_buf[window, 2 * h * HEAD_DIM : 2 * (h + 1) * HEAD_DIM],
            preferred_element_type=jnp.float32,
        )

    known = keys - group_rows(len(GROUPS) - 1)[1]

    def attend_early(t, g):
        start, size = group_rows(g)
        for h in range(heads):
            early[h, start : start + size] = attention(t, g, h, 0, known)

    def attend(t, g):
        start, size = group_rows(g)
        rows = slice(start, start + size)
        mixed = []
        for h in range(heads):
            if g < len(GROUPS) - 1:
                both = early[h, rows] + attention(t, g, h, known, keys)
            else:
                both = attention(t, g, h, 0, keys)
            mixed.append((both[:, :HEAD_DIM] / both[:, HEAD_DIM:]).astype(jnp.bfloat16))
        mixed = jnp.concatenate(mixed, axis=1)
        for j in range(ny):
            columns = slice(j * share, (j + 1) * share)
            terms[t, j, rows] = jnp.dot(
                mixed, wout[:, columns], preferred_element_type=jnp.float32
            ).astype(jnp.bfloat16)
        for c in GROUPS[g]:
            far_copy(t, c, FAR_RIGHT, across, to_right).start()
            far_copy(t, c, FAR_LEFT, across, to_left).start()
        for c in GROUPS[g]:
            plain(t, c)

    def plain(t, c):
        near_copy(t, c, PLAIN_RIGHT, right, to_right).start()
        near_copy(t, c, PLAIN_LEFT, left, to_left).start()

    def combine(t, c):
        for far, near, who, device in (
            (FAR_RIGHT, SUM_RIGHT, right, to_right),
            (FAR_LEFT, SUM_LEFT, left, to_left),
        ):
            far_copy(t, c, far, who, device).wait_recv()
            rows = half_of(c, far == FAR_LEFT)
            terms[t, who, rows] = (
                terms[t, who, rows].astype(jnp.float32) + far_buf[t, rows].astype(jnp.float32)
            ).astype(jnp.bfloat16)
            near_copy(t, c, near, who, device).start()

    def finish(t, c):
        for kind in (PLAIN_RIGHT, PLAIN_LEFT, SUM_RIGHT, SUM_LEFT):
            device = to_right if kind in (PLAIN_RIGHT, SUM_RIGHT) else to_left
            near_copy(t, c, kind, y, device).wait_recv()
        rows = rows_of(c)
        total = terms[t, y, rows].astype(jnp.float32)
        total += near_buf[t, 0, rows].astype(jnp.float32)
        total += near_buf[t, 1, rows].astype(jnp.float32)
        gate = mod[2, :, pl.ds(pl.multiple_of(y * share, 128), share)]
        y_buf[t, rows] = (rows_buf[t, y, rows].astype(jnp.float32) + gate * total).astype(
            jnp.bfloat16
        )
        shift_copy(t, c).start()

    def arrive(t, c):
        shift_copy(t - 1, c).wait_recv()
        gather_send(t, c)

    first_core = lax.rem(section, 2) == 0
    loads[0].wait()

    @pl.when(first_core)
    def _():
        for c in range(chunks):
            gather_send(0, c)

    for load in loads[1:2]:
        load.wait()
    slot = lax.rem(4 * sections - section, 4)
    for place, later in ((0, 1), (patch + text, 2), (2 * patch + text, 3)):
        which = jnp.full((patch, inner), order_ref[lax.rem(slot + later, 4)], jnp.int32)
        picked = [stale[s, text : text + patch].astype(jnp.float32) for s in range(2)]
        for k in range(1, 4):
            source = slice(text + k * patch, text + (k + 1) * patch)
            for s in range(2):
                picked[s] = jnp.where(which == k, stale[s, source].astype(jnp.float32), picked[s])
        k_buf[place : place + patch] = picked[0].astype(jnp.bfloat16)
        for h in range(heads):
            v_buf[place : place + patch, 2 * h * HEAD_DIM : (2 * h + 1) * HEAD_DIM] = picked[1][
                :, h * HEAD_DIM : (h + 1) * HEAD_DIM
            ].astype(jnp.bfloat16)
    k_buf[patch : patch + text] = stale[0, :text]
    for h in range(heads):
        v_buf[patch : patch + text, 2 * h * HEAD_DIM : (2 * h + 1) * HEAD_DIM] = stale[
            1, :text, h * HEAD_DIM : (h + 1) * HEAD_DIM
        ]
        v_buf[:, (2 * h + 1) * HEAD_DIM : 2 * (h + 1) * HEAD_DIM] = jnp.ones(
            (keys + patch, HEAD_DIM), jnp.bfloat16
        )

    @pl.when(jnp.logical_not(first_core))
    def _():
        pl.semaphore_wait(go_sem, 1)
        for c in range(chunks):
            gather_send(0, c)

    everything = range(chunks)
    for t in range(TICKS):
        for c in everything:
            gather_pass(t, c)
            if t == 0 and c == 0:

                @pl.when(first_core)
                def _():
                    pl.semaphore_signal(go_sem, inc=1, device_id=to_ahead, device_id_type=MESH)

        if t == 1:

            @pl.when(lax.rem(section, sections // 4) == 0)
            def _():
                pl.semaphore_signal(go_sem, inc=1, device_id=to_ahead, device_id_type=MESH)

        if t == 0:
            for load in loads[2:]:
                load.wait()
        for g in range(len(GROUPS)):
            project(t, g)
            if g < len(GROUPS) - 1:
                attend_early(t, g)
        if t == 1:

            @pl.when(lax.rem(section, sections // 4) == 1)
            def _():
                pl.semaphore_wait(go_sem, 1)

        for g in range(len(GROUPS)):
            attend(t, g)
        for c in everything:
            combine(t, c)
        if t + 1 < TICKS:

            @pl.when(jnp.logical_not(first_core))
            def _():
                for c in everything:
                    arrive(t + 1, c)

        for c in everything:
            finish(t, c)
        if t + 1 < TICKS:

            @pl.when(first_core)
            def _():
                for c in everything:
                    arrive(t + 1, c)

    for t in range(TICKS):
        for c in everything:
            own_copy(t, c, OWN_RIGHT, y, to_right).wait_send()
            own_copy(t, c, OWN_LEFT, y, to_left).wait_send()
            pass_copy(t, c, PASS_RIGHT, left, to_right).wait_send()
            pass_copy(t, c, PASS_LEFT, right, to_left).wait_send()
            far_copy(t, c, FAR_RIGHT, across, to_right).wait_send()
            far_copy(t, c, FAR_LEFT, across, to_left).wait_send()
            near_copy(t, c, PLAIN_RIGHT, right, to_right).wait_send()
            near_copy(t, c, PLAIN_LEFT, left, to_left).wait_send()
            near_copy(t, c, SUM_RIGHT, right, to_right).wait_send()
            near_copy(t, c, SUM_LEFT, left, to_left).wait_send()
            shift_copy(t, c).wait_send()
    for c in everything:
        shift_copy(TICKS - 1, c).wait_recv()


def solution(mesh):
    sections = mesh.shape["section"]

    def per_device(state, modulation, w_qkv, w_out, stale_kv, patch_order, text_count):
        patch, share = state.shape[1:]
        width = modulation.shape[2]
        inner = w_out.shape[1]
        keys = stale_kv.shape[2]
        heads = inner // HEAD_DIM
        bf16 = jnp.bfloat16
        anywhere = pl.BlockSpec(memory_space=pl.ANY)
        chunks = len(spans_of(patch))
        flops = TICKS * 2 * patch * inner * (3 * width + 2 * keys + width)
        out, fresh = pl.pallas_call(
            functools.partial(kernel, sections),
            out_shape=(
                pltpu.VMEM((patch, share), bf16),
                pltpu.VMEM((TICKS, 2, patch, inner), bf16),
            ),
            in_specs=[pl.BlockSpec(memory_space=pltpu.SMEM)] * 2 + [anywhere] * 5,
            out_specs=(pl.BlockSpec(memory_space=pltpu.VMEM),) * 2,
            scratch_shapes=[
                pltpu.VMEM((TICKS, 4, patch, share), bf16),
                pltpu.VMEM((TICKS, 4, patch, share), bf16),
                pltpu.VMEM((TICKS, patch, share), bf16),
                pltpu.VMEM((TICKS, 2, patch, share), bf16),
                pltpu.VMEM((TICKS, patch, share), bf16),
                pltpu.VMEM((3, 1, width), jnp.float32),
                pltpu.VMEM((width, 3 * inner), bf16),
                pltpu.VMEM((inner, width), bf16),
                pltpu.VMEM((2, keys, inner), bf16),
                pltpu.VMEM((patch, width), bf16),
                pltpu.VMEM((heads, patch, 2 * HEAD_DIM), jnp.float32),
                pltpu.VMEM((patch, inner), bf16),
                pltpu.VMEM((keys + patch, inner), bf16),
                pltpu.VMEM((keys + patch, 2 * heads * HEAD_DIM), bf16),
                pltpu.SemaphoreType.DMA((16,)),
                pltpu.SemaphoreType.DMA((TICKS, chunks, KINDS)),
                pltpu.SemaphoreType.DMA((TICKS, chunks, KINDS)),
                pltpu.SemaphoreType.REGULAR,
            ],
            compiler_params=pltpu.CompilerParams(
                collective_id=0, has_side_effects=True, vmem_limit_bytes=48 * 2**20
            ),
            cost_estimate=pl.CostEstimate(
                flops=flops, bytes_accessed=14 * 2**20, transcendentals=TICKS * patch * keys * heads
            ),
        )(
            pltpu.with_memory_space_constraint(patch_order, pltpu.HBM),
            text_count,
            *(
                pltpu.with_memory_space_constraint(value, pltpu.HBM)
                for value in (
                    state[0],
                    jnp.transpose(modulation, (1, 0, 2)),
                    jnp.transpose(w_qkv[0], (1, 0, 2)),
                    w_out[0],
                    stale_kv[0],
                )
            ),
        )
        return out[None], fresh[None]

    return jax.shard_map(
        per_device,
        mesh=mesh,
        in_specs=(
            P("section", None, "head"),
            P("section", None, None),
            P("section", None, None, "head"),
            P("section", "head", None),
            P("section", None, None, "head"),
            P(),
            P(),
        ),
        out_specs=(P("section", None, "head"), P("section", None, None, None, "head")),
        check_vma=False,
    )
```

```python
import functools

import jax
import jax.numpy as jnp
from jax import lax
from jax.experimental import pallas as pl
from jax.experimental.pallas import tpu as pltpu
from jax.sharding import PartitionSpec as P

MESH = pl.DeviceIdType.MESH
HEAD_DIM = 128
TICKS = 2
EPSILON = 1e-06
SPANS = ((0, 64), (64, 64), (128, 64), (192, 64))
GROUPS = ((0, 1), (2, 3))


(
    OWN_RIGHT,
    OWN_LEFT,
    PASS_RIGHT,
    PASS_LEFT,
    FAR_RIGHT,
    FAR_LEFT,
    PLAIN_RIGHT,
    PLAIN_LEFT,
    SUM_RIGHT,
    SUM_LEFT,
    SHIFT,
    KINDS,
) = range(12)


def spans_of(patch):
    return [(start * patch // 256, size * patch // 256) for start, size in SPANS]


def kernel(
    sections,
    order_ref,
    count_ref,
    state_ref,
    mod_ref,
    wqkv_ref,
    wout_ref,
    stale_ref,
    out_ref,
    fresh_ref,
    rows_buf,
    terms,
    far_buf,
    near_buf,
    y_buf,
    mod,
    wqkv,
    wout,
    stale,
    h_buf,
    early,
    q_buf,
    k_buf,
    v_buf,
    local_sem,
    send_sem,
    recv_sem,
    go_sem,
):
    section = lax.axis_index("section")
    y = lax.axis_index("head")
    ny = 4
    right, left, across = lax.rem(y + 1, ny), lax.rem(y + 3, ny), lax.rem(y + 2, ny)
    behind = lax.rem(section + sections - 1, sections)
    ahead = lax.rem(section + 1, sections)
    to_right, to_left, to_ahead = (section, right), (section, left), (ahead, y)

    patch, share = state_ref.shape
    inner = wout_ref.shape[0]
    heads = inner // HEAD_DIM
    keys = stale_ref.shape[1]
    text = keys - 4 * patch
    width = ny * share
    spans = spans_of(patch)
    chunks = len(spans)

    loads = [
        (state_ref, rows_buf.at[0, y]),
        (stale_ref, stale),
        (mod_ref, mod),
    ]
    for s in range(3):
        loads.append((wqkv_ref.at[s], wqkv.at[:, s * inner : (s + 1) * inner]))
    loads.append((wout_ref, wout))
    loads = [
        pltpu.make_async_copy(source, target, local_sem.at[i])
        for i, (source, target) in enumerate(loads)
    ]
    for load in loads:
        load.start()

    barrier = pltpu.get_barrier_semaphore()
    for target in (to_right, to_left, (behind, y)):
        pl.semaphore_signal(barrier, inc=1, device_id=target, device_id_type=MESH)
    pl.semaphore_wait(barrier, 3)

    def rows_of(c):
        start, size = spans[c]
        return slice(start, start + size)

    def half_of(c, second):
        start, size = spans[c]
        start += second * (size // 2)
        return slice(start, start + size // 2)

    def remote(t, c, kind, source, target, device):
        return pltpu.make_async_remote_copy(
            src_ref=source,
            dst_ref=target,
            send_sem=send_sem.at[t, c, kind],
            recv_sem=recv_sem.at[t, c, kind],
            device_id=device,
            device_id_type=MESH,
        )

    def own_copy(t, c, kind, who, device):
        ref = rows_buf.at[t, who, rows_of(c)]
        source = state_ref.at[rows_of(c)] if t == 0 else ref
        return remote(t, c, kind, source, ref, device)

    def pass_copy(t, c, kind, who, device):
        ref = rows_buf.at[t, who, half_of(c, kind == PASS_LEFT)]
        return remote(t, c, kind, ref, ref, device)

    def far_copy(t, c, kind, who, device):
        rows = half_of(c, kind == FAR_LEFT)
        return remote(t, c, kind, terms.at[t, who, rows], far_buf.at[t, rows], device)

    def near_copy(t, c, kind, who, device):
        side = 0 if kind in (PLAIN_RIGHT, SUM_RIGHT) else 1
        rows = half_of(c, kind in (PLAIN_RIGHT, SUM_LEFT))
        return remote(t, c, kind, terms.at[t, who, rows], near_buf.at[t, side, rows], device)

    def shift_copy(t, c):
        if t + 1 < TICKS:
            target = rows_buf.at[t + 1, y, rows_of(c)]
        else:
            target = out_ref.at[rows_of(c)]
        return remote(t, c, SHIFT, y_buf.at[t, rows_of(c)], target, to_ahead)

    def gather_send(t, c):
        own_copy(t, c, OWN_RIGHT, y, to_right).start()
        own_copy(t, c, OWN_LEFT, y, to_left).start()

    def gather_pass(t, c):
        own_copy(t, c, OWN_RIGHT, left, to_right).wait_recv()
        pass_copy(t, c, PASS_RIGHT, left, to_right).start()
        own_copy(t, c, OWN_LEFT, right, to_left).wait_recv()
        pass_copy(t, c, PASS_LEFT, right, to_left).start()

    def group_rows(g):
        start = spans[GROUPS[g][0]][0]
        return start, sum(spans[c][1] for c in GROUPS[g])

    def project(t, g):
        for c in GROUPS[g]:
            pass_copy(t, c, PASS_RIGHT, across, to_right).wait_recv()
            pass_copy(t, c, PASS_LEFT, across, to_left).wait_recv()
        start, size = group_rows(g)
        rows = slice(start, start + size)
        for first in range(start, start + size, 16):
            few = slice(first, first + 16)
            parts = [rows_buf[t, j, few].astype(jnp.float32) for j in range(ny)]
            centre = mean_of(parts)
            parts = [part - centre for part in parts]
            factor = lax.rsqrt(mean_of([part * part for part in parts]) + EPSILON)
            for j in range(ny):
                columns = slice(j * share, (j + 1) * share)
                normed = parts[j] * factor * (1.0 + mod[1, :, columns]) + mod[0, :, columns]
                h_buf[few, columns] = normed.astype(jnp.bfloat16)
        sums = jnp.dot(h_buf[rows], wqkv[...], preferred_element_type=jnp.float32)
        place = slice(fresh_row(t) + start, fresh_row(t) + start + size)
        for h in range(heads):
            columns = slice(h * HEAD_DIM, (h + 1) * HEAD_DIM)
            q_buf[rows, columns] = head_norm(sums[:, columns])
            fresh_key = head_norm(sums[:, inner + h * HEAD_DIM : inner + (h + 1) * HEAD_DIM])
            k_buf[place, columns] = fresh_key
            fresh_ref[t, 0, rows, columns] = fresh_key
            first = 2 * inner + h * HEAD_DIM
            fresh_value = sums[:, first : first + HEAD_DIM].astype(jnp.bfloat16)
            v_buf[place, 2 * h * HEAD_DIM : (2 * h + 1) * HEAD_DIM] = fresh_value
            fresh_ref[t, 1, rows, columns] = fresh_value

    def mean_of(parts):
        folded = None
        for part in parts:
            for k in range(share // HEAD_DIM):
                piece = part[:, k * HEAD_DIM : (k + 1) * HEAD_DIM]
                folded = piece if folded is None else folded + piece
        return jnp.sum(folded, axis=-1, keepdims=True) * (1.0 / width)

    def head_norm(value):
        square = jnp.mean(value * value, axis=-1, keepdims=True)
        return (value * lax.rsqrt(square + EPSILON)).astype(jnp.bfloat16)

    def fresh_row(t):
        return text + 3 * patch + t * patch

    def attention(t, g, h, first, last):
        start, size = group_rows(g)
        columns = slice(h * HEAD_DIM, (h + 1) * HEAD_DIM)
        window = slice(t * patch + first, t * patch + last)
        scores = lax.dot_general(
            q_buf[start : start + size, columns],
            k_buf[window, columns],
            (((1,), (1,)), ((), ())),
            preferred_element_type=jnp.float32,
        )
        weights = jnp.exp(scores * HEAD_DIM ** (-0.5))
        text_at = patch if t == 0 else 0
        if first <= text_at < last:
            position = lax.broadcasted_iota(jnp.int32, (size, text), 1)
            alive = position < count_ref[0]
            pieces = [jnp.where(alive, weights[:, text_at : text_at + text], 0.0)]
            if text_at:
                pieces.insert(0, weights[:, :text_at])
            pieces.append(weights[:, text_at + text :])
            weights = jnp.concatenate(pieces, axis=1)
        return jnp.dot(
            weights.astype(jnp.bfloat16),
            v_buf[window, 2 * h * HEAD_DIM : 2 * (h + 1) * HEAD_DIM],
            preferred_element_type=jnp.float32,
        )

    known = keys - group_rows(len(GROUPS) - 1)[1]

    def attend_early(t, g):
        start, size = group_rows(g)
        for h in range(heads):
            early[h, start : start + size] = attention(t, g, h, 0, known)

    def attend(t, g):
        start, size = group_rows(g)
        rows = slice(start, start + size)
        mixed = []
        for h in range(heads):
            if g < len(GROUPS) - 1:
                both = early[h, rows] + attention(t, g, h, known, keys)
            else:
                both = attention(t, g, h, 0, keys)
            mixed.append((both[:, :HEAD_DIM] / both[:, HEAD_DIM:]).astype(jnp.bfloat16))
        mixed = jnp.concatenate(mixed, axis=1)
        for j in range(ny):
            columns = slice(j * share, (j + 1) * share)
            terms[t, j, rows] = jnp.dot(
                mixed, wout[:, columns], preferred_element_type=jnp.float32
            ).astype(jnp.bfloat16)
        for c in GROUPS[g]:
            far_copy(t, c, FAR_RIGHT, across, to_right).start()
            far_copy(t, c, FAR_LEFT, across, to_left).start()
        for c in GROUPS[g]:
            plain(t, c)

    def plain(t, c):
        near_copy(t, c, PLAIN_RIGHT, right, to_right).start()
        near_copy(t, c, PLAIN_LEFT, left, to_left).start()

    def combine(t, c):
        for far, near, who, device in (
            (FAR_RIGHT, SUM_RIGHT, right, to_right),
            (FAR_LEFT, SUM_LEFT, left, to_left),
        ):
            far_copy(t, c, far, who, device).wait_recv()
            rows = half_of(c, far == FAR_LEFT)
            terms[t, who, rows] = (
                terms[t, who, rows].astype(jnp.float32) + far_buf[t, rows].astype(jnp.float32)
            ).astype(jnp.bfloat16)
            near_copy(t, c, near, who, device).start()

    def finish(t, c):
        for kind in (PLAIN_RIGHT, PLAIN_LEFT, SUM_RIGHT, SUM_LEFT):
            device = to_right if kind in (PLAIN_RIGHT, SUM_RIGHT) else to_left
            near_copy(t, c, kind, y, device).wait_recv()
        rows = rows_of(c)
        total = terms[t, y, rows].astype(jnp.float32)
        total += near_buf[t, 0, rows].astype(jnp.float32)
        total += near_buf[t, 1, rows].astype(jnp.float32)
        gate = mod[2, :, pl.ds(pl.multiple_of(y * share, 128), share)]
        y_buf[t, rows] = (rows_buf[t, y, rows].astype(jnp.float32) + gate * total).astype(
            jnp.bfloat16
        )
        shift_copy(t, c).start()

    def arrive(t, c):
        shift_copy(t - 1, c).wait_recv()
        gather_send(t, c)

    first_core = lax.rem(section, 2) == 0

    @pl.when(first_core)
    def _():
        for c in range(chunks):
            gather_send(0, c)

    for load in loads[:2]:
        load.wait()
    slot = lax.rem(4 * sections - section, 4)
    for place, later in ((0, 1), (patch + text, 2), (2 * patch + text, 3)):
        which = jnp.full((patch, inner), order_ref[lax.rem(slot + later, 4)], jnp.int32)
        picked = [stale[s, text : text + patch].astype(jnp.float32) for s in range(2)]
        for k in range(1, 4):
            source = slice(text + k * patch, text + (k + 1) * patch)
            for s in range(2):
                picked[s] = jnp.where(which == k, stale[s, source].astype(jnp.float32), picked[s])
        k_buf[place : place + patch] = picked[0].astype(jnp.bfloat16)
        for h in range(heads):
            v_buf[place : place + patch, 2 * h * HEAD_DIM : (2 * h + 1) * HEAD_DIM] = picked[1][
                :, h * HEAD_DIM : (h + 1) * HEAD_DIM
            ].astype(jnp.bfloat16)
    k_buf[patch : patch + text] = stale[0, :text]
    for h in range(heads):
        v_buf[patch : patch + text, 2 * h * HEAD_DIM : (2 * h + 1) * HEAD_DIM] = stale[
            1, :text, h * HEAD_DIM : (h + 1) * HEAD_DIM
        ]
        v_buf[:, (2 * h + 1) * HEAD_DIM : 2 * (h + 1) * HEAD_DIM] = jnp.ones(
            (keys + patch, HEAD_DIM), jnp.bfloat16
        )

    @pl.when(jnp.logical_not(first_core))
    def _():
        pl.semaphore_wait(go_sem, 1)
        for c in range(chunks):
            gather_send(0, c)

    everything = range(chunks)
    for t in range(TICKS):
        for c in everything:
            gather_pass(t, c)
            if t == 0 and c == 0:

                @pl.when(first_core)
                def _():
                    pl.semaphore_signal(go_sem, inc=1, device_id=to_ahead, device_id_type=MESH)

        if t == 1:

            @pl.when(lax.rem(section, sections // 4) == 0)
            def _():
                pl.semaphore_signal(go_sem, inc=1, device_id=to_ahead, device_id_type=MESH)

        if t == 0:
            for load in loads[2:]:
                load.wait()
        for g in range(len(GROUPS)):
            project(t, g)
            if g < len(GROUPS) - 1:
                attend_early(t, g)
        if t == 1:

            @pl.when(lax.rem(section, sections // 4) == 1)
            def _():
                pl.semaphore_wait(go_sem, 1)

        for g in range(len(GROUPS)):
            attend(t, g)
        for c in everything:
            combine(t, c)
        if t + 1 < TICKS:

            @pl.when(jnp.logical_not(first_core))
            def _():
                for c in everything:
                    arrive(t + 1, c)

        for c in everything:
            finish(t, c)
        if t + 1 < TICKS:

            @pl.when(first_core)
            def _():
                for c in everything:
                    arrive(t + 1, c)

    for t in range(TICKS):
        for c in everything:
            own_copy(t, c, OWN_RIGHT, y, to_right).wait_send()
            own_copy(t, c, OWN_LEFT, y, to_left).wait_send()
            pass_copy(t, c, PASS_RIGHT, left, to_right).wait_send()
            pass_copy(t, c, PASS_LEFT, right, to_left).wait_send()
            far_copy(t, c, FAR_RIGHT, across, to_right).wait_send()
            far_copy(t, c, FAR_LEFT, across, to_left).wait_send()
            near_copy(t, c, PLAIN_RIGHT, right, to_right).wait_send()
            near_copy(t, c, PLAIN_LEFT, left, to_left).wait_send()
            near_copy(t, c, SUM_RIGHT, right, to_right).wait_send()
            near_copy(t, c, SUM_LEFT, left, to_left).wait_send()
            shift_copy(t, c).wait_send()
    for c in everything:
        shift_copy(TICKS - 1, c).wait_recv()


def solution(mesh):
    sections = mesh.shape["section"]

    def per_device(state, modulation, w_qkv, w_out, stale_kv, patch_order, text_count):
        patch, share = state.shape[1:]
        width = modulation.shape[2]
        inner = w_out.shape[1]
        keys = stale_kv.shape[2]
        heads = inner // HEAD_DIM
        bf16 = jnp.bfloat16
        anywhere = pl.BlockSpec(memory_space=pl.ANY)
        chunks = len(spans_of(patch))
        flops = TICKS * 2 * patch * inner * (3 * width + 2 * keys + width)
        out, fresh = pl.pallas_call(
            functools.partial(kernel, sections),
            out_shape=(
                pltpu.VMEM((patch, share), bf16),
                pltpu.VMEM((TICKS, 2, patch, inner), bf16),
            ),
            in_specs=[pl.BlockSpec(memory_space=pltpu.SMEM)] * 2 + [anywhere] * 5,
            out_specs=(pl.BlockSpec(memory_space=pltpu.VMEM),) * 2,
            scratch_shapes=[
                pltpu.VMEM((TICKS, 4, patch, share), bf16),
                pltpu.VMEM((TICKS, 4, patch, share), bf16),
                pltpu.VMEM((TICKS, patch, share), bf16),
                pltpu.VMEM((TICKS, 2, patch, share), bf16),
                pltpu.VMEM((TICKS, patch, share), bf16),
                pltpu.VMEM((3, 1, width), jnp.float32),
                pltpu.VMEM((width, 3 * inner), bf16),
                pltpu.VMEM((inner, width), bf16),
                pltpu.VMEM((2, keys, inner), bf16),
                pltpu.VMEM((patch, width), bf16),
                pltpu.VMEM((heads, patch, 2 * HEAD_DIM), jnp.float32),
                pltpu.VMEM((patch, inner), bf16),
                pltpu.VMEM((keys + patch, inner), bf16),
                pltpu.VMEM((keys + patch, 2 * heads * HEAD_DIM), bf16),
                pltpu.SemaphoreType.DMA((16,)),
                pltpu.SemaphoreType.DMA((TICKS, chunks, KINDS)),
                pltpu.SemaphoreType.DMA((TICKS, chunks, KINDS)),
                pltpu.SemaphoreType.REGULAR,
            ],
            compiler_params=pltpu.CompilerParams(
                collective_id=0, has_side_effects=True, vmem_limit_bytes=48 * 2**20
            ),
            cost_estimate=pl.CostEstimate(
                flops=flops, bytes_accessed=14 * 2**20, transcendentals=TICKS * patch * keys * heads
            ),
        )(
            pltpu.with_memory_space_constraint(patch_order, pltpu.HBM),
            text_count,
            *(
                pltpu.with_memory_space_constraint(value, pltpu.HBM)
                for value in (
                    state[0],
                    jnp.transpose(modulation, (1, 0, 2)),
                    jnp.transpose(w_qkv[0], (1, 0, 2)),
                    w_out[0],
                    stale_kv[0],
                )
            ),
        )
        return out[None], fresh[None]

    return jax.shard_map(
        per_device,
        mesh=mesh,
        in_specs=(
            P("section", None, "head"),
            P("section", None, None),
            P("section", None, None, "head"),
            P("section", "head", None),
            P("section", None, None, "head"),
            P(),
            P(),
        ),
        out_specs=(P("section", None, "head"), P("section", None, None, None, "head")),
        check_vma=False,
    )
```
